256 devices in a mesh: space: 128 (over y_hi, x, z, core), chan: 2 (over y_lo).
Axes of the slice: x: 4, y: 4 (y_hi: 2, y_lo: 2; y = y_hi * 2 + y_lo), z: 8, core: 2. Of those that a mesh axis runs over, the one named last changes fastest.
Arguments:
- features: bfloat16 [256, 16, 32, 256], P('space'), may hold values from -24 to 24
- kernel: bfloat16 [256, 27, 512], P(None, None, 'chan'), may hold values from -0.078125 to 0.078125
- cotangent: bfloat16 [256, 16, 32, 512], P('space', None, None, 'chan'), may hold values from -6 to 6
Outputs:
- input_grad: bfloat16 [256, 16, 32, 256], P('space', None, None, 'chan')
- kernel_grad: float32 [256, 27, 512], P('space', None, 'chan')
The draws below stay inside these ranges and needn't reach their ends.
All inputs are finite; a program needn't handle non-finite values.
Results may differ from the reference program's by a relative error of at most 0.012.
Values may be sent and summed in bfloat16 or wider, within the bound.
A program may use at most 192 MiB of HBM per device.

```python
import jax
import jax.numpy as jnp
from jax import lax

CIN = 256
COUT = 512
SY = 16
SZ = 32
NX = 256


def raised(drawn, rng, source, target, blocks, factor):
    owner, partner = [(jnp.arange(drawn.shape[axis_at]) // (drawn.shape[axis_at] // blocks)).reshape([-1 if axis == axis_at else 1 for axis in range(drawn.ndim)]) for axis_at in (source, target)]
    chosen = jax.random.permutation(rng, blocks)[partner]
    strong = (owner == chosen) | (owner == (partner + blocks // 2) % blocks)
    return jnp.where(strong, factor * drawn, drawn)


def steps_of(stream_key, shape, cuts, low, largest):
    def one(dim, blocks):
        draws = jax.random.uniform(jax.random.fold_in(jax.random.fold_in(stream_key, 6), dim), (blocks,), jnp.float32, low / len(cuts), largest / len(cuts))
        return jnp.repeat(jnp.exp(draws), shape[dim] // blocks).reshape((-1,) + (1,) * (len(shape) - dim - 1))

    loudness = one(*cuts[0])
    for cut in cuts[1:]:
        loudness = loudness * one(*cut)
    return loudness


def noise(rng, extent, scale, reach, split=(), kind=jnp.bfloat16):
    array = jax.random.normal(rng, extent, jnp.float32) * scale
    if len(split) > 0:
        array = steps_of(rng, extent, split, -0.22, 0.18) * array
    return jnp.clip(array, min=-reach, max=reach).astype(kind)


def noise_with(stream_key, shape, deviation, limit, split, heavy, kind=jnp.bfloat16):
    entries = deviation * jax.random.normal(stream_key, shape, jnp.float32)
    if split:
        entries = entries * steps_of(stream_key, shape, split, -0.22, 0.18)
    return jnp.clip(raised(entries, jax.random.fold_in(stream_key, 3), *heavy), -limit, limit).astype(kind)


def setup_inputs(seed: int = 0) -> dict:
    keys = jax.random.split(jax.random.key(seed), 4)
    return {
        "features": noise_with(keys[0], (NX, SY, SZ, CIN), 1.0, 24.0, ((0, 128),), (0, 3, 128, 5.5)),
        "kernel": noise(keys[1], (CIN, 27, COUT), (27 * CIN) ** -0.5, 0.078125, ((2, 2),)),
        "cotangent": noise(keys[2], (NX, SY, SZ, COUT), 1.0, 6.0, ((0, 128), (3, 2))),
    }


OFFSETS = [(a, b, c) for a in (-1, 0, 1) for b in (-1, 0, 1) for c in (-1, 0, 1)]


def columns(block, sign):
    depth = block.shape[0] - 2
    pieces = []
    for a, b, c in OFFSETS:
        part = block[1 + sign * a:1 + sign * a + depth]
        part = jnp.roll(part, -sign * b, axis=1)
        part = jnp.roll(part, -sign * c, axis=2)
        pieces.append(part)
    stacked = jnp.stack(pieces, axis=-2)
    return stacked.reshape(depth * block.shape[1] * block.shape[2], 27, block.shape[3])


def wrap_pad(field):
    return jnp.concatenate([field[-1:], field, field[:1]], axis=0)


def reference(features, kernel, cotangent):
    kernel32 = kernel.astype(jnp.float32)
    padded = wrap_pad(features)

    def forward_plane(total, index):
        block = lax.dynamic_slice_in_dim(padded, index, 3, 0)
        cols = columns(block, 1).astype(jnp.float32)
        pre = jnp.einsum('ntc,ctk->nk', cols, kernel32)
        sig = jax.nn.sigmoid(pre)
        upstream = lax.dynamic_slice_in_dim(cotangent, index, 1, 0).reshape(pre.shape).astype(jnp.float32)
        pre_grad = (upstream * sig * (1.0 + pre * (1.0 - sig))).astype(jnp.bfloat16)
        total = total + jnp.einsum('ntc,nk->ctk', cols, pre_grad.astype(jnp.float32))
        return total, pre_grad.reshape(SY, SZ, COUT)

    start = jnp.zeros((CIN, 27, COUT), jnp.float32)
    kernel_grad, grads = lax.scan(forward_plane, start, jnp.arange(NX, dtype=jnp.int32))
    grad_pad = wrap_pad(grads)

    def backward_plane(index):
        block = lax.dynamic_slice_in_dim(grad_pad, index, 3, 0)
        cols = columns(block, -1).astype(jnp.float32)
        result = jnp.einsum('ntk,ctk->nc', cols, kernel32)
        return result.astype(jnp.bfloat16).reshape(SY, SZ, CIN)

    input_grad = lax.map(backward_plane, jnp.arange(NX, dtype=jnp.int32))
    return input_grad, kernel_grad
```

```python
import jax
import jax.numpy as jnp
from jax import lax
from jax.experimental import pallas as pl
from jax.experimental.pallas import tpu as pltpu
from jax.sharding import PartitionSpec as P

BF = jnp.bfloat16
F32 = jnp.float32
MESH = pl.DeviceIdType.MESH

NY, NX, NZ = 2, 4, 8
SY, SZ, C = 16, 32, 256
CELLS = SY * SZ
HALO = CELLS + 2 * SZ
HALF = 128

Y_SET = (0, 1, 2, 3, 4)
X_SET = (5, 6, 7, 8)
ORDER = (0, 5, 1, 6, 2, 7, 3, 8, 4)

NT = (((1,), (1,)), ((), ()))


def device(y, x, z, core):
    return ((y * NX + x) * NZ + z) * 2 + core


def spread(plane, sign, store):
    wide = plane.reshape(SY, SZ, C)
    wide32 = wide.astype(F32)
    for ci, c in enumerate((-1, 0, 1)):
        part = wide if c == 0 else pltpu.roll(wide32, (sign * c) % SZ, 1).astype(BF)
        store(ci, part.reshape(CELLS, C))


def fused(
    feat, kern, cot, ig_out, kg_out,
    kv, fb, ct, fs, pr, ps, ft, acc, pkx, pky,
    xr1, s1x, yr2, yr1, s1y, xr2, s2x, s2y, zsx, zsy, zrx, zry,
    own, igs, igr, permx, permy, sel,
    loc, f_s, f_r, g_s, g_r, x1_s, x1_r, y2_s, y2_r, y1_s, y1_r, x2_s, x2_r,
    zx_s, zx_r, zy_s, zy_r, i_s, i_r,
):
    s = lax.axis_index("space")
    l = lax.axis_index("chan")
    core = lax.rem(s, 2)
    z = lax.rem(lax.div(s, 2), NZ)
    x = lax.rem(lax.div(s, 2 * NZ), NX)
    y = lax.div(s, 2 * NZ * NX)
    count = 2 * NZ * NX * NY

    partner = (device(y, x, z, 1 - core), l)
    outer = (lax.rem(s + 2 * core - 1 + count, count), l)
    x_peers = [(device(y, lax.rem(x + d, NX), z, core), l) for d in range(1, NX)]
    y_peer = (device(1 - y, x, z, core), l)
    z_peers = [(device(y, x, lax.rem(z + d, NZ), core), l) for d in range(1, NZ)]
    chan_peer = (s, 1 - l)

    sent = []

    def send(src, dst, ss, rs, to):
        copy = pltpu.make_async_remote_copy(
            src_ref=src, dst_ref=dst, send_sem=ss, recv_sem=rs, device_id=to, device_id_type=MESH
        )
        copy.start()
        sent.append(copy)
        return copy

    first = 1 + 2 * core
    here = pl.ds(first, 2)
    load_f = pltpu.make_async_copy(feat, fb.at[here], loc.at[0])
    load_f.start()
    load_k = []
    for n, t0 in enumerate((9, 0, 18)):
        part = pl.ds(t0, 9)
        load_k.append(pltpu.make_async_copy(kern.at[part], kv.at[part], loc.at[1 + n]))
        load_k[-1].start()
    load_c = pltpu.make_async_copy(cot, ct, loc.at[4])
    load_c.start()

    barrier = pltpu.get_barrier_semaphore()
    greeted = [partner, outer, *x_peers, y_peer, *z_peers, chan_peer]
    for peer in greeted:
        pl.semaphore_signal(barrier, inc=1, device_id=peer, device_id_type=MESH)

    row = lax.broadcasted_iota(jnp.int32, (HALF, C), 0)
    col = lax.broadcasted_iota(jnp.int32, (HALF, C), 1)
    sel[...] = jnp.where((row >> 1) * 4 + core * 2 + (row & 1) == col, 1.0, 0.0).astype(BF)
    row = lax.broadcasted_iota(jnp.int32, (C, C), 0)
    col = lax.broadcasted_iota(jnp.int32, (C, C), 1)
    for perm, groups in ((permx, len(X_SET)), (permy, len(Y_SET))):
        q = row & 31
        a = jnp.where(q >= 2 * groups, 1, 0) + jnp.where(q >= 4 * groups, 1, 0)
        rest = q - 2 * groups * a
        source = ((rest >> 1) * 3 + a) * 16 + (row >> 5) * 2 + (rest & 1)
        perm[...] = jnp.where((source == col) & (q < 6 * groups), 1.0, 0.0).astype(BF)
    s2x[...] = jnp.zeros_like(s2x)
    s2y[...] = jnp.zeros_like(s2y)

    pl.semaphore_wait(barrier, len(greeted))

    f_out = send(feat.at[core], fb.at[5 * (1 - core)], f_s.at[0], f_r.at[0], outer)
    f_pair = send(feat, fb.at[here], f_s.at[1], f_r.at[1], partner)

    def spread_f(slot, plane):
        def store(ci, part):
            fs[ci, slot, SZ : SZ + CELLS, :] = part
            fs[ci, slot, 0:SZ, :] = part[CELLS - SZ :]
            fs[ci, slot, SZ + CELLS :, :] = part[:SZ]

        spread(plane, -1, store)

    def spread_g(g):
        def store(ci, part):
            ps[ci, g, SZ : SZ + CELLS, :] = part
            ps[ci, g, 0:SZ, :] = part[CELLS - SZ :]
            ps[ci, g, SZ + CELLS :, :] = part[:SZ]

        spread(pr[g], 1, store)

    def taps_f(slot):
        return jnp.concatenate(
            [fs[c, slot, b * SZ : b * SZ + CELLS, :] for b in range(3) for c in range(3)], axis=1
        )

    def times(slot, t0):
        return jnp.dot(taps_f(slot), kv[pl.ds(t0, 9)].reshape(9 * C, C), preferred_element_type=F32)

    load_f.wait()
    for i in range(2):
        spread_f(1 + i, fb[first + i])
    load_k[0].wait()
    for i in range(2):
        acc[i] = times(1 + i, 9)
    load_k[1].wait()
    acc[1] += times(1, 0)
    load_k[2].wait()
    acc[0] += times(2, 18)
    load_c.wait()

    def epilogue(i, g):
        def body(n, carry):
            rows = pl.ds(pl.multiple_of(n * 64, 64), 64)
            pre = acc[i, rows, :]
            sig = 1.0 / (1.0 + jnp.exp(-pre))
            pr[g, rows, :] = (ct[i, rows, :].astype(F32) * sig * (1.0 + pre * (1.0 - sig))).astype(BF)
            return carry

        lax.fori_loop(0, CELLS // 64, body, 0)

    def features_t(g):
        cols = pl.ds(pl.multiple_of(g * CELLS, CELLS), CELLS)
        ft[:, cols] = lax.dot_general(sel[...], fb[g], NT, preferred_element_type=F32).astype(BF)

    f_pair.wait_recv()
    side = 3 * (1 - core)
    spread_f(side, fb[2 * core + side])
    inner = 1 - core
    acc[inner] += times(side, 18 * (1 - core))
    g_inner = 2 + core
    epilogue(inner, g_inner)
    g_pair0 = send(pr.at[g_inner], pr.at[g_inner], g_s.at[0], g_r.at[0], partner)
    for g in range(1, 5):
        features_t(g)

    f_out.wait_recv()
    f_relay = send(fb.at[5 * core], fb.at[5 * core], f_s.at[2], f_r.at[2], partner)
    spread_f(3 * core, fb[5 * core])
    acc[core] += times(3 * core, 18 * core)
    g_outer = 1 + 3 * core
    epilogue(core, g_outer)
    g_pair1 = send(pr.at[g_outer], pr.at[g_outer], g_s.at[1], g_r.at[1], partner)
    g_out = send(pr.at[g_outer], pr.at[5 * (1 - core)], g_s.at[2], g_r.at[2], outer)
    spread_g(g_inner)
    spread_g(g_outer)
    features_t(5 * core)
    f_relay.wait_recv()
    features_t(5 * (1 - core))
    g_pair0.wait_recv()
    spread_g(3 - core)
    g_pair1.wait_recv()
    spread_g(4 - 3 * core)

    first_x, first_y = {}, {}
    for g in ORDER:
        b, c = divmod(g, 3)
        left = jnp.concatenate([ft[:, a * CELLS : (a + 4) * CELLS] for a in range(3)], axis=0)
        right = jnp.concatenate(
            [ps[c, p, (2 - b) * SZ : (2 - b) * SZ + CELLS, :] for p in range(1, 5)], axis=0
        )
        part = jnp.dot(left, right, preferred_element_type=F32).astype(BF).reshape(3, NY, NX, 16, C)
        if g in X_SET:
            n = X_SET.index(g)
            for k in range(NX):
                pkx[n, k] = part[:, :, k]
            first_x[n] = [
                send(pkx.at[n, lax.rem(x + d, NX)], xr1.at[n, d - 1], x1_s.at[n, d - 1], x1_r.at[n, d - 1], x_peers[d - 1])
                for d in range(1, NX)
            ]
        else:
            n = Y_SET.index(g)
            for k in range(NY):
                pky[n, k] = part[:, k]
            first_y[n] = send(pky.at[n, 1 - y], yr1.at[n], y1_s.at[n], y1_r.at[n], y_peer)

    second_x, second_y = {}, {}

    def sum_x1(n):
        for copy in first_x[n]:
            copy.wait_recv()
        total = pkx[n, x].astype(F32)
        for d in range(NX - 1):
            total = total + xr1[n, d].astype(F32)
        total = total.astype(BF)
        for k in range(NY):
            s1x[n, k] = total[:, k]
        second_x[n] = send(s1x.at[n, 1 - y], yr2.at[n], y2_s.at[n], y2_r.at[n], y_peer)

    def sum_y1(n):
        first_y[n].wait_recv()
        total = (pky[n, y].astype(F32) + yr1[n].astype(F32)).astype(BF)
        for k in range(NX):
            s1y[n, k] = total[:, k]
        second_y[n] = [
            send(s1y.at[n, lax.rem(x + d, NX)], xr2.at[n, d - 1], x2_s.at[n, d - 1], x2_r.at[n, d - 1], x_peers[d - 1])
            for d in range(1, NX)
        ]

    def sum_x2(n):
        second_x[n].wait_recv()
        total = s1x[n, y].astype(F32) + yr2[n].astype(F32)
        s2x[n * 48 : (n + 1) * 48, :] = total.astype(BF).reshape(48, C)

    def sum_y2(n):
        for copy in second_y[n]:
            copy.wait_recv()
        total = s1y[n, x].astype(F32)
        for d in range(NX - 1):
            total = total + xr2[n, d].astype(F32)
        s2y[n * 48 : (n + 1) * 48, :] = total.astype(BF).reshape(48, C)

    def last(perm, rows, zs, zr, ss, rs):
        zs[...] = jnp.dot(perm[...], rows[...], preferred_element_type=F32).astype(BF).reshape(NZ, 32, C)
        return [
            send(zs.at[lax.rem(z + d, NZ)], zr.at[d - 1], ss.at[d - 1], rs.at[d - 1], z_peers[d - 1])
            for d in range(1, NZ)
        ]

    def input_plane(i):
        total = None
        for a in range(3):
            left = jnp.concatenate(
                [ps[c, first + i - (a - 1), (2 - b) * SZ : (2 - b) * SZ + CELLS, :] for b in range(3) for c in range(3)],
                axis=1,
            )
            right = jnp.concatenate([kv[9 * a + u] for u in range(9)], axis=1)
            term = lax.dot_general(left, right, NT, preferred_element_type=F32)
            total = term if total is None else total + term
        low, high = total[:, :HALF], total[:, HALF:]
        own[i] = jnp.where(l == 0, low, high)
        igs[i] = jnp.where(l == 0, high, low).astype(BF)
        return send(igs.at[i], igr.at[i], i_s.at[i], i_r.at[i], chan_peer)

    g_out.wait_recv()
    spread_g(5 * core)
    ig0 = input_plane(0)
    for n in range(3):
        sum_y1(n)
    for n in range(2):
        sum_x1(n)
    ig1 = input_plane(1)
    for n in range(3, 5):
        sum_y1(n)
    for n in range(2, 4):
        sum_x1(n)
    for n in range(4):
        sum_x2(n)
    last_x = last(permx, s2x, zsx, zrx, zx_s, zx_r)
    for n in range(5):
        sum_y2(n)
    last_y = last(permy, s2y, zsy, zry, zy_s, zy_r)

    for i, copy in enumerate((ig0, ig1)):
        copy.wait_recv()
        ig_out[i] = (own[i] + igr[i].astype(F32)).astype(BF)

    def final(copies, zs, zr):
        total = zs[z].astype(F32)
        for d in range(NZ - 1):
            copies[d].wait_recv()
            total = total + zr[d].astype(F32)
        return total

    total = final(last_x, zsx, zrx)
    for a in range(3):
        kg_out[a * 18 + 10 : a * 18 + 18, :] = total[a * 8 : a * 8 + 8]
    total = final(last_y, zsy, zry)
    for a in range(3):
        kg_out[a * 18 : a * 18 + 10, :] = total[a * 10 : a * 10 + 10]

    for copy in sent:
        copy.wait_send()


def shards(features, kernel, cotangent):
    taps = jnp.transpose(kernel, (1, 0, 2))
    dma = pltpu.SemaphoreType.DMA
    nx, ny = len(X_SET), len(Y_SET)
    pairs = [(3,), (3,), (nx, 3), (nx,), (ny,), (ny, 3), (7,), (7,), (2,)]
    sems = [dma((5,))]
    for shape in pairs:
        sems += [dma(shape), dma(shape)]
    whole = pl.BlockSpec(memory_space=pl.ANY)
    vmem = pl.BlockSpec(memory_space=pltpu.VMEM)
    input_grad, kernel_grad = pl.pallas_call(
        fused,
        name="conv_grads",
        out_shape=(
            jax.ShapeDtypeStruct((2, CELLS, HALF), BF),
            jax.ShapeDtypeStruct((54, C), F32),
        ),
        in_specs=[whole] * 3,
        out_specs=(vmem, vmem),
        scratch_shapes=[
            pltpu.VMEM((27, C, C), BF),
            pltpu.VMEM((6, CELLS, C), BF),
            pltpu.VMEM((2, CELLS, C), BF),
            pltpu.VMEM((3, 4, HALO, C), BF),
            pltpu.VMEM((6, CELLS, C), BF),
            pltpu.VMEM((3, 6, HALO, C), BF),
            pltpu.VMEM((HALF, 6 * CELLS), BF),
            pltpu.VMEM((2, CELLS, C), F32),
            pltpu.VMEM((nx, NX, 3, NY, 16, C), BF),
            pltpu.VMEM((ny, NY, 3, NX, 16, C), BF),
            pltpu.VMEM((nx, 3, 3, NY, 16, C), BF),
            pltpu.VMEM((nx, NY, 3, 16, C), BF),
            pltpu.VMEM((nx, 3, 16, C), BF),
            pltpu.VMEM((ny, 3, NX, 16, C), BF),
            pltpu.VMEM((ny, NX, 3, 16, C), BF),
            pltpu.VMEM((ny, 3, 3, 16, C), BF),
            pltpu.VMEM((C, C), BF),
            pltpu.VMEM((C, C), BF),
            pltpu.VMEM((NZ, 32, C), BF),
            pltpu.VMEM((NZ, 32, C), BF),
            pltpu.VMEM((NZ - 1, 32, C), BF),
            pltpu.VMEM((NZ - 1, 32, C), BF),
            pltpu.VMEM((2, CELLS, HALF), F32),
            pltpu.VMEM((2, CELLS, HALF), BF),
            pltpu.VMEM((2, CELLS, HALF), BF),
            pltpu.VMEM((C, C), BF),
            pltpu.VMEM((C, C), BF),
            pltpu.VMEM((HALF, C), BF),
            *sems,
        ],
        compiler_params=pltpu.CompilerParams(
            collective_id=0, has_side_effects=True, vmem_limit_bytes=56 * 1024 * 1024
        ),
        cost_estimate=pl.CostEstimate(flops=11_000_000_000, bytes_accessed=6_000_000, transcendentals=300_000),
    )(features.reshape(2, CELLS, C), taps, cotangent.reshape(2, CELLS, C))
    return (
        input_grad.reshape(2, SY, SZ, HALF),
        jnp.transpose(kernel_grad.reshape(27, 2, C), (1, 0, 2)),
    )


def solution(mesh):
    placed = (P("space", None, None, None), P(None, None, "chan"), P("space", None, None, "chan"))
    return jax.shard_map(
        shards,
        mesh=mesh,
        in_specs=placed,
        out_specs=(P("space", None, None, "chan"), P("space", None, "chan")),
        check_vma=False,
    )
```

```python
import jax
import jax.numpy as jnp
from jax import lax
from jax.experimental import pallas as pl
from jax.experimental.pallas import tpu as pltpu
from jax.sharding import PartitionSpec as P

BF = jnp.bfloat16
F32 = jnp.float32
MESH = pl.DeviceIdType.MESH

NY, NX, NZ = 2, 4, 8
SY, SZ, C = 16, 32, 256
CELLS = SY * SZ
HALO = CELLS + 2 * SZ
HALF = 128

Y_SET = (0, 1, 2, 3, 4)
X_SET = (5, 6, 7, 8)
ORDER = (0, 5, 1, 6, 2, 7, 3, 8, 4)

NT = (((1,), (1,)), ((), ()))


def block_rows(groups):
    return -(-6 * len(groups) // 16) * 16


BX, BY = block_rows(X_SET), block_rows(Y_SET)


def device(y, x, z, core):
    return ((y * NX + x) * NZ + z) * 2 + core


def spread(plane, sign, store):
    wide = plane.reshape(SY, SZ, C)
    wide32 = wide.astype(F32)
    for ci, c in enumerate((-1, 0, 1)):
        part = wide if c == 0 else pltpu.roll(wide32, (sign * c) % SZ, 1).astype(BF)
        store(ci, part.reshape(CELLS, C))


def fused(
    feat, kern, cot, ig_out, kg_out,
    kv, fb, ct, fs, pr, ps, ft, acc, pkx, pky,
    xr1, s1x, yr2, yr1, s1y, xr2, s2x, s2y, zsx, zsy, zrx, zry,
    own, igs, igr, permx, permy, sel,
    ig_sum, kg_sum,
    loc, f_s, f_r, g_s, g_r, x1_s, x1_r, y2_s, y2_r, y1_s, y1_r, x2_s, x2_r,
    zx_s, zx_r, zy_s, zy_r, i_s, i_r,
):
    s = lax.axis_index("space")
    l = lax.axis_index("chan")
    core = lax.rem(s, 2)
    z = lax.rem(lax.div(s, 2), NZ)
    x = lax.rem(lax.div(s, 2 * NZ), NX)
    y = lax.div(s, 2 * NZ * NX)
    count = 2 * NZ * NX * NY

    partner = (device(y, x, z, 1 - core), l)
    outer = (lax.rem(s + 2 * core - 1 + count, count), l)
    x_peers = [(device(y, lax.rem(x + d, NX), z, core), l) for d in range(1, NX)]
    y_peer = (device(1 - y, x, z, core), l)
    z_peers = [(device(y, x, lax.rem(z + d, NZ), core), l) for d in range(1, NZ)]
    chan_peer = (s, 1 - l)

    sent = []

    def send(src, dst, ss, rs, to):
        copy = pltpu.make_async_remote_copy(
            src_ref=src, dst_ref=dst, send_sem=ss, recv_sem=rs, device_id=to, device_id_type=MESH
        )
        copy.start()
        sent.append(copy)
        return copy

    first = 1 + 2 * core
    here = pl.ds(first, 2)
    load_f = pltpu.make_async_copy(feat, fb.at[here], loc.at[0])
    load_f.start()
    load_k = []
    for n, t0 in enumerate((9, 0, 18)):
        part = pl.ds(t0, 9)
        load_k.append(pltpu.make_async_copy(kern.at[part], kv.at[part], loc.at[1 + n]))
    for copy in load_k:
        copy.start()
    load_c = pltpu.make_async_copy(cot, ct, loc.at[4])
    load_c.start()

    barrier = pltpu.get_barrier_semaphore()
    greeted = [partner, outer, *x_peers, y_peer, *z_peers, chan_peer]
    for peer in greeted:
        pl.semaphore_signal(barrier, inc=1, device_id=peer, device_id_type=MESH)

    pl.semaphore_wait(barrier, len(greeted))

    f_out = send(feat.at[core], fb.at[5 * (1 - core)], f_s.at[0], f_r.at[0], outer)
    f_pair = send(feat, fb.at[here], f_s.at[1], f_r.at[1], partner)

    def spread_f(slot, plane):
        def store(ci, part):
            fs[ci, slot, SZ : SZ + CELLS, :] = part
            fs[ci, slot, 0:SZ, :] = part[CELLS - SZ :]
            fs[ci, slot, SZ + CELLS :, :] = part[:SZ]

        spread(plane, -1, store)

    def spread_g(g):
        def store(ci, part):
            ps[ci, g, SZ : SZ + CELLS, :] = part
            ps[ci, g, 0:SZ, :] = part[CELLS - SZ :]
            ps[ci, g, SZ + CELLS :, :] = part[:SZ]

        spread(pr[g], 1, store)

    def taps_f(slot):
        return jnp.concatenate(
            [fs[c, slot, b * SZ : b * SZ + CELLS, :] for b in range(3) for c in range(3)], axis=1
        )

    def times(slot, t0):
        return jnp.dot(taps_f(slot), kv[pl.ds(t0, 9)].reshape(9 * C, C), preferred_element_type=F32)

    row = lax.broadcasted_iota(jnp.int32, (HALF, C), 0)
    col = lax.broadcasted_iota(jnp.int32, (HALF, C), 1)
    sel[...] = jnp.where((row >> 1) * 4 + core * 2 + (row & 1) == col, 1.0, 0.0).astype(BF)

    load_f.wait()
    for i in range(2):
        spread_f(1 + i, fb[first + i])
    load_k[0].wait()
    for i in range(2):
        acc[i] = times(1 + i, 9)
    load_k[1].wait()
    acc[1] += times(1, 0)
    load_k[2].wait()
    acc[0] += times(2, 18)
    load_c.wait()

    def epilogue(i, g):
        def body(n, carry):
            rows = pl.ds(pl.multiple_of(n * 64, 64), 64)
            pre = acc[i, rows, :]
            sig = 1.0 / (1.0 + jnp.exp(-pre))
            pr[g, rows, :] = (ct[i, rows, :].astype(F32) * sig * (1.0 + pre * (1.0 - sig))).astype(BF)
            return carry

        lax.fori_loop(0, CELLS // 64, body, 0)

    def features_t(g):
        cols = pl.ds(pl.multiple_of(g * CELLS, CELLS), CELLS)
        ft[:, cols] = lax.dot_general(sel[...], fb[g], NT, preferred_element_type=F32).astype(BF)

    f_pair.wait_recv()
    side = 3 * (1 - core)
    spread_f(side, fb[2 * core + side])
    inner = 1 - core
    acc[inner] += times(side, 18 * (1 - core))
    g_inner = 2 + core
    epilogue(inner, g_inner)
    g_pair0 = send(pr.at[g_inner], pr.at[g_inner], g_s.at[0], g_r.at[0], partner)

    f_out.wait_recv()
    f_relay = send(fb.at[5 * core], fb.at[5 * core], f_s.at[2], f_r.at[2], partner)
    spread_f(3 * core, fb[5 * core])
    acc[core] += times(3 * core, 18 * core)
    g_outer = 1 + 3 * core
    epilogue(core, g_outer)
    g_pair1 = send(pr.at[g_outer], pr.at[g_outer], g_s.at[1], g_r.at[1], partner)
    g_out = send(pr.at[g_outer], pr.at[5 * (1 - core)], g_s.at[2], g_r.at[2], outer)
    spread_g(g_inner)
    spread_g(g_outer)
    for g in range(1, 5):
        features_t(g)
    features_t(5 * core)
    f_relay.wait_recv()
    features_t(5 * (1 - core))
    g_pair0.wait_recv()
    spread_g(3 - core)
    g_pair1.wait_recv()
    spread_g(4 - 3 * core)

    first_x, first_y = {}, {}
    for g in ORDER:
        b, c = divmod(g, 3)
        left = jnp.concatenate([ft[:, a * CELLS : (a + 4) * CELLS] for a in range(3)], axis=0)
        right = jnp.concatenate(
            [ps[c, p, (2 - b) * SZ : (2 - b) * SZ + CELLS, :] for p in range(1, 5)], axis=0
        )
        part = jnp.dot(left, right, preferred_element_type=F32).astype(BF)
        part = part.reshape(3, NY, NX, 16, C)
        if g in X_SET:
            n = X_SET.index(g)
            for k in range(NX):
                pkx[n, k] = part[:, :, k]
            first_x[n] = [
                send(pkx.at[n, lax.rem(x + d, NX)], xr1.at[n, d - 1], x1_s.at[n, d - 1], x1_r.at[n, d - 1], x_peers[d - 1])
                for d in range(1, NX)
            ]
        else:
            n = Y_SET.index(g)
            for k in range(NY):
                pky[n, k] = part[:, k]
            first_y[n] = send(pky.at[n, 1 - y], yr1.at[n], y1_s.at[n], y1_r.at[n], y_peer)

    second_x, second_y = {}, {}

    def sum_x1(n):
        for copy in first_x[n]:
            copy.wait_recv()
        total = pkx[n, x].astype(F32)
        for d in range(NX - 1):
            total = total + xr1[n, d].astype(F32)
        total = total.astype(BF)
        for k in range(NY):
            s1x[n, k] = total[:, k]
        second_x[n] = send(s1x.at[n, 1 - y], yr2.at[n], y2_s.at[n], y2_r.at[n], y_peer)

    def sum_y1(n):
        first_y[n].wait_recv()
        total = (pky[n, y].astype(F32) + yr1[n].astype(F32)).astype(BF)
        for k in range(NX):
            s1y[n, k] = total[:, k]
        second_y[n] = [
            send(s1y.at[n, lax.rem(x + d, NX)], xr2.at[n, d - 1], x2_s.at[n, d - 1], x2_r.at[n, d - 1], x_peers[d - 1])
            for d in range(1, NX)
        ]

    def sum_x2(n):
        second_x[n].wait_recv()
        total = s1x[n, y].astype(F32) + yr2[n].astype(F32)
        s2x[n * 48 : (n + 1) * 48, :] = total.astype(BF).reshape(48, C)

    def sum_y2(n):
        for copy in second_y[n]:
            copy.wait_recv()
        total = s1y[n, x].astype(F32)
        for d in range(NX - 1):
            total = total + xr2[n, d].astype(F32)
        s2y[n * 48 : (n + 1) * 48, :] = total.astype(BF).reshape(48, C)

    def ordered(perm, rows, out):
        out[...] = jnp.dot(perm[...], rows[...], preferred_element_type=F32).astype(BF).reshape(out.shape)

    def last(perm, rows, zs, zr, ss, rs):
        ordered(perm, rows, zs)
        return [
            send(zs.at[lax.rem(z + d, NZ)], zr.at[d - 1], ss.at[d - 1], rs.at[d - 1], z_peers[d - 1])
            for d in range(1, NZ)
        ]

    def input_plane(i):
        total = None
        for a in range(3):
            left = jnp.concatenate(
                [ps[c, first + i - (a - 1), (2 - b) * SZ : (2 - b) * SZ + CELLS, :] for b in range(3) for c in range(3)],
                axis=1,
            )
            right = jnp.concatenate([kv[9 * a + u] for u in range(9)], axis=1)
            term = lax.dot_general(left, right, NT, preferred_element_type=F32)
            total = term if total is None else total + term
        low, high = total[:, :HALF], total[:, HALF:]
        own[i] = jnp.where(l == 0, low, high)
        igs[i] = jnp.where(l == 0, high, low).astype(BF)

    row = lax.broadcasted_iota(jnp.int32, (C, C), 0)
    col = lax.broadcasted_iota(jnp.int32, (C, C), 1)
    for perm, groups, shift in ((permx, X_SET, BX), (permy, Y_SET, BY)):
        n = len(groups)
        block = lax.div(row, shift)
        q = row - block * shift
        a = jnp.where(q >= 2 * n, 1, 0) + jnp.where(q >= 4 * n, 1, 0)
        rest = q - 2 * n * a
        source = ((rest >> 1) * 3 + a) * 16 + block * 2 + (rest & 1)
        hot = jnp.where((source == col) & (q < 6 * n), 1.0, 0.0).astype(BF)
        perm[...] = hot[: 8 * shift]
    s2x[...] = jnp.zeros_like(s2x)
    s2y[...] = jnp.zeros_like(s2y)

    g_out.wait_recv()
    spread_g(5 * core)
    input_plane(0)
    for n in range(3):
        sum_y1(n)
    for n in range(2):
        sum_x1(n)
    input_plane(1)
    for n in range(2, 4):
        sum_x1(n)
    for n in range(3, 5):
        sum_y1(n)
    ig_copies = [send(igs.at[i], igr.at[i], i_s.at[i], i_r.at[i], chan_peer) for i in range(2)]
    for n in range(4):
        sum_x2(n)
    copies_x = last(permx, s2x, zsx, zrx, zx_s, zx_r)
    for n in range(5):
        sum_y2(n)
    copies_y = last(permy, s2y, zsy, zry, zy_s, zy_r)

    def final(groups, copies, mine, taken):
        total = mine.astype(F32)
        for d, copy in enumerate(copies):
            copy.wait_recv()
            total = total + taken[d].astype(F32)
        n = len(groups)
        for a in range(3):
            kg_sum[a * 9 + groups[0] : a * 9 + groups[0] + n] = total[a * 2 * n : (a + 1) * 2 * n].reshape(n, 2, C)

    out_copies = []
    for i, copy in enumerate(ig_copies):
        copy.wait_recv()
        ig_sum[i] = (own[i] + igr[i].astype(F32)).astype(BF)
        out_copies.append(pltpu.make_async_copy(ig_sum.at[i], ig_out.at[i], loc.at[5 + i]))
        out_copies[-1].start()
    final(Y_SET, copies_y, zsy[z], zry)
    final(X_SET, copies_x, zsx[z], zrx)
    out_copies.append(pltpu.make_async_copy(kg_sum, kg_out, loc.at[7]))
    out_copies[-1].start()
    for copy in out_copies:
        copy.wait()

    for copy in sent:
        copy.wait_send()


def copy_out(ig, kg, ig_out, kg_out, ig_held, kg_held, sem):
    steps = []
    for i in range(2):
        for h in range(2):
            part = (i, pl.ds(h * (CELLS // 2), CELLS // 2))
            steps.append((ig.at[part], ig_held.at[part], ig_out.at[part]))
    steps.append((kg, kg_held, kg_out))
    copies = [
        (pltpu.make_async_copy(a, b, sem.at[0, n]), pltpu.make_async_copy(b, c, sem.at[1, n]))
        for n, (a, b, c) in enumerate(steps)
    ]
    for inward, _ in copies:
        inward.start()
    for inward, outward in copies:
        inward.wait()
        outward.start()
    for _, outward in copies:
        outward.wait()


def shards(features, kernel, cotangent):
    taps = jnp.transpose(kernel, (1, 0, 2))
    dma = pltpu.SemaphoreType.DMA
    nx, ny = len(X_SET), len(Y_SET)
    pairs = [(3,), (3,), (nx, 3), (nx,), (ny,), (ny, 3), (7,), (7,), (2,)]
    sems = [dma((8,))]
    for shape in pairs:
        sems += [dma(shape), dma(shape)]
    whole = pl.BlockSpec(memory_space=pl.ANY)
    input_grad, kernel_grad = pl.pallas_call(
        fused,
        name="conv_grads",
        out_shape=(
            jax.ShapeDtypeStruct((2, CELLS, HALF), BF),
            jax.ShapeDtypeStruct((27, 2, C), F32),
        ),
        in_specs=[whole] * 3,
        out_specs=(whole, whole),
        scratch_shapes=[
            pltpu.VMEM((27, C, C), BF),
            pltpu.VMEM((6, CELLS, C), BF),
            pltpu.VMEM((2, CELLS, C), BF),
            pltpu.VMEM((3, 4, HALO, C), BF),
            pltpu.VMEM((6, CELLS, C), BF),
            pltpu.VMEM((3, 6, HALO, C), BF),
            pltpu.VMEM((HALF, 6 * CELLS), BF),
            pltpu.VMEM((2, CELLS, C), F32),
            pltpu.VMEM((nx, NX, 3, NY, 16, C), BF),
            pltpu.VMEM((ny, NY, 3, NX, 16, C), BF),
            pltpu.VMEM((nx, 3, 3, NY, 16, C), BF),
            pltpu.VMEM((nx, NY, 3, 16, C), BF),
            pltpu.VMEM((nx, 3, 16, C), BF),
            pltpu.VMEM((ny, 3, NX, 16, C), BF),
            pltpu.VMEM((ny, NX, 3, 16, C), BF),
            pltpu.VMEM((ny, 3, 3, 16, C), BF),
            pltpu.VMEM((C, C), BF),
            pltpu.VMEM((C, C), BF),
            pltpu.VMEM((NZ, BX, C), BF),
            pltpu.VMEM((NZ, BY, C), BF),
            pltpu.VMEM((NZ - 1, BX, C), BF),
            pltpu.VMEM((NZ - 1, BY, C), BF),
            pltpu.VMEM((2, CELLS, HALF), F32),
            pltpu.VMEM((2, CELLS, HALF), BF),
            pltpu.VMEM((2, CELLS, HALF), BF),
            pltpu.VMEM((8 * BX, C), BF),
            pltpu.VMEM((8 * BY, C), BF),
            pltpu.VMEM((HALF, C), BF),
            pltpu.VMEM((2, CELLS, HALF), BF),
            pltpu.VMEM((27, 2, C), F32),
            *sems,
        ],
        compiler_params=pltpu.CompilerParams(
            collective_id=0, has_side_effects=True, vmem_limit_bytes=58 * 1024 * 1024
        ),
        cost_estimate=pl.CostEstimate(flops=11_000_000_000, bytes_accessed=6_000_000, transcendentals=300_000),
    )(features.reshape(2, CELLS, C), taps, cotangent.reshape(2, CELLS, C))
    input_grad, kernel_grad = pl.pallas_call(
        copy_out,
        name="copy_out",
        out_shape=(
            jax.ShapeDtypeStruct((2, CELLS, HALF), BF),
            jax.ShapeDtypeStruct((27, 2, C), F32),
        ),
        in_specs=[whole] * 2,
        out_specs=(whole, whole),
        scratch_shapes=[
            pltpu.VMEM((2, CELLS, HALF), BF),
            pltpu.VMEM((27, 2, C), F32),
            dma((2, 5)),
        ],
        compiler_params=pltpu.CompilerParams(vmem_limit_bytes=60 * 1024 * 1024),
    )(input_grad, kernel_grad)
    return (
        input_grad.reshape(2, SY, SZ, HALF),
        jnp.transpose(kernel_grad, (1, 0, 2)),
    )


def solution(mesh):
    placed = (P("space", None, None, None), P(None, None, "chan"), P("space", None, None, "chan"))
    return jax.shard_map(
        shards,
        mesh=mesh,
        in_specs=placed,
        out_specs=(P("space", None, None, "chan"), P("space", None, "chan")),
        check_vma=False,
    )
```

```python
import jax
import jax.numpy as jnp
from jax import lax
from jax.experimental import pallas as pl
from jax.experimental.pallas import tpu as pltpu
from jax.sharding import PartitionSpec as P

BF = jnp.bfloat16
F32 = jnp.float32
MESH = pl.DeviceIdType.MESH

NY, NX, NZ = 2, 4, 8
SY, SZ, C = 16, 32, 256
CELLS = SY * SZ
HALO = CELLS + 2 * SZ
HALF = 128

Y_SET = (0, 1, 2, 3, 4)
X_SET = (5, 6, 7, 8)

NT = (((1,), (1,)), ((), ()))


def block_rows(groups):
    return -(-6 * len(groups) // 16) * 16


BX, BY = block_rows(X_SET), block_rows(Y_SET)


def device(y, x, z, core):
    return ((y * NX + x) * NZ + z) * 2 + core


def spread(plane, sign, store):
    wide = plane.reshape(SY, SZ, C)
    wide32 = wide.astype(F32)
    for ci, c in enumerate((-1, 0, 1)):
        part = wide if c == 0 else pltpu.roll(wide32, (sign * c) % SZ, 1).astype(BF)
        store(ci, part.reshape(CELLS, C))


def fused(
    feat, kern, cot, ig_out, kg_out,
    kv, fb, ct, fs, pr, ps, ft, acc, pk,
    xr1, s1x, yr2, yr1, s1y, xr2, s2x, s2y, zsx, zsy, zrx, zry,
    own, igs, igr, permx, permy, sel,
    ig_sum, kg_sum,
    loc, f_s, f_r, g_s, g_r, x1_s, x1_r, y2_s, y2_r, y1_s, y1_r, x2_s, x2_r,
    zx_s, zx_r, zy_s, zy_r, i_s, i_r,
):
    s = lax.axis_index("space")
    l = lax.axis_index("chan")
    core = lax.rem(s, 2)
    z = lax.rem(lax.div(s, 2), NZ)
    x = lax.rem(lax.div(s, 2 * NZ), NX)
    y = lax.div(s, 2 * NZ * NX)
    count = 2 * NZ * NX * NY

    partner = (device(y, x, z, 1 - core), l)
    outer = (lax.rem(s + 2 * core - 1 + count, count), l)
    x_peers = [(device(y, lax.rem(x + d, NX), z, core), l) for d in range(1, NX)]
    y_peer = (device(1 - y, x, z, core), l)
    z_peers = [(device(y, x, lax.rem(z + d, NZ), core), l) for d in range(1, NZ)]
    chan_peer = (s, 1 - l)

    sent = []

    def send(src, dst, ss, rs, to):
        copy = pltpu.make_async_remote_copy(
            src_ref=src, dst_ref=dst, send_sem=ss, recv_sem=rs, device_id=to, device_id_type=MESH
        )
        sent.append(copy)
        return copy

    def start(*args):
        copy = send(*args)
        copy.start()
        return copy

    first = 1 + 2 * core
    here = pl.ds(first, 2)
    load_f = pltpu.make_async_copy(feat, fb.at[here], loc.at[0])
    load_f.start()
    load_k = []
    for n, t0 in enumerate((9, 0, 18)):
        part = pl.ds(t0, 9)
        load_k.append(pltpu.make_async_copy(kern.at[part], kv.at[part], loc.at[1 + n]))
    for copy in load_k:
        copy.start()
    load_c = pltpu.make_async_copy(cot, ct, loc.at[4])
    load_c.start()

    barrier = pltpu.get_barrier_semaphore()
    greeted = [partner, outer, *x_peers, y_peer, *z_peers, chan_peer]
    for peer in greeted:
        pl.semaphore_signal(barrier, inc=1, device_id=peer, device_id_type=MESH)

    pl.semaphore_wait(barrier, len(greeted))

    f_out = start(feat.at[core], fb.at[5 * (1 - core)], f_s.at[0], f_r.at[0], outer)
    f_pair = start(feat, fb.at[here], f_s.at[1], f_r.at[1], partner)

    def spread_f(slot, plane):
        def store(ci, part):
            fs[ci, slot, SZ : SZ + CELLS, :] = part
            fs[ci, slot, 0:SZ, :] = part[CELLS - SZ :]
            fs[ci, slot, SZ + CELLS :, :] = part[:SZ]

        spread(plane, -1, store)

    def spread_g(g):
        def store(ci, part):
            part = part.reshape(SY, SZ, C)
            ps[ci, g, 1 : SY + 1] = part
            ps[ci, g, 0] = part[SY - 1]
            ps[ci, g, SY + 1] = part[0]

        spread(pr[g], 1, store)

    def taps_g(c, g, b):
        return ps[c, g, pl.ds(2 - b, SY)].reshape(CELLS, C)

    def taps_f(slot):
        return jnp.concatenate(
            [fs[c, slot, b * SZ : b * SZ + CELLS, :] for b in range(3) for c in range(3)], axis=1
        )

    def times(slot, t0):
        return jnp.dot(taps_f(slot), kv[pl.ds(t0, 9)].reshape(9 * C, C), preferred_element_type=F32)

    row = lax.broadcasted_iota(jnp.int32, (HALF, C), 0)
    col = lax.broadcasted_iota(jnp.int32, (HALF, C), 1)
    sel[...] = jnp.where((row >> 1) * 4 + core * 2 + (row & 1) == col, 1.0, 0.0).astype(BF)

    load_f.wait()
    for i in range(2):
        spread_f(1 + i, fb[first + i])
    acc[...] = jnp.zeros_like(acc)

    def epilogue(i, g):
        def body(n, carry):
            rows = pl.ds(pl.multiple_of(n * 64, 64), 64)
            pre = acc[i, rows, :]
            sig = 1.0 / (1.0 + jnp.exp(-pre))
            pr[g, rows, :] = (ct[i, rows, :].astype(F32) * sig * (1.0 + pre * (1.0 - sig))).astype(BF)
            return carry

        lax.fori_loop(0, CELLS // 64, body, 0)

    def features_t(g):
        cols = pl.ds(pl.multiple_of(g * CELLS, CELLS), CELLS)
        ft[:, cols] = lax.dot_general(sel[...], fb[g], NT, preferred_element_type=F32).astype(BF)

    inner = 1 - core
    side = 3 * inner
    g_inner, g_outer, g_far = 2 + core, 1 + 3 * core, 5 * core
    g_side = 2 * core + side
    f_relay = send(fb.at[g_far], fb.at[g_far], f_s.at[2], f_r.at[2], partner)
    g_pair0 = send(pr.at[g_inner], pr.at[g_inner], g_s.at[0], g_r.at[0], partner)
    g_pair1 = send(pr.at[g_outer], pr.at[g_outer], g_s.at[1], g_r.at[1], partner)
    g_out = send(pr.at[g_outer], pr.at[5 * inner], g_s.at[2], g_r.at[2], outer)

    def forward(n, carry):
        late = n // 4
        m = n % 4
        slot = (1 - late) * (1 + n % 2) + late * ((1 - m) * side + m * 3 * core)
        t0 = (1 - late) * (9 + (n // 2) * (18 * (n % 2) - 9)) + late * 18 * ((1 - m) * inner + m * core)
        i = (1 - late) * ((n % 2 + n // 2) % 2) + late * ((1 - m) * inner + m * core)

        @pl.when(n == 0)
        def _():
            load_k[0].wait()

        @pl.when(n == 2)
        def _():
            load_k[1].wait()

        @pl.when(n == 3)
        def _():
            load_k[2].wait()

        @pl.when(n == 4)
        def _():
            load_c.wait()
            f_pair.wait_recv()

        @pl.when(n == 5)
        def _():
            f_out.wait_recv()
            f_relay.start()

        @pl.when(n >= 4)
        def _():
            spread_f(slot, fb[2 * core + slot])

        acc[i] += times(slot, t0)

        @pl.when(n >= 4)
        def _():
            epilogue(i, first + i)

        @pl.when(n == 4)
        def _():
            g_pair0.start()

        @pl.when(n == 5)
        def _():
            g_pair1.start()
            g_out.start()

        return carry

    lax.fori_loop(0, 6, forward, 0)
    spread_g(g_inner)
    spread_g(g_outer)
    for g in range(1, 5):
        features_t(g)
    features_t(5 * core)
    f_relay.wait_recv()
    features_t(5 * (1 - core))
    g_pair0.wait_recv()
    spread_g(3 - core)
    g_pair1.wait_recv()
    spread_g(4 - 3 * core)

    def remote(src, dst, ss, rs, to):
        return pltpu.make_async_remote_copy(
            src_ref=src, dst_ref=dst, send_sem=ss, recv_sem=rs, device_id=to, device_id_type=MESH
        )

    def x1(n, d):
        mine = pk.at[2 * n + 1, :, :, lax.rem(x + d, NX)]
        return remote(mine, xr1.at[n, d - 1], x1_s.at[n, d - 1], x1_r.at[n, d - 1], x_peers[d - 1])

    def y1(n):
        return remote(pk.at[2 * n, :, 1 - y], yr1.at[n], y1_s.at[n], y1_r.at[n], y_peer)

    def x2(n, d):
        mine = s1y.at[n, lax.rem(x + d, NX)]
        return remote(mine, xr2.at[n, d - 1], x2_s.at[n, d - 1], x2_r.at[n, d - 1], x_peers[d - 1])

    def y2(n):
        return remote(s1x.at[n, 1 - y], yr2.at[n], y2_s.at[n], y2_r.at[n], y_peer)

    def terms(u, carry):
        odd = u % 2
        n = u // 2
        g = n + len(Y_SET) * odd
        b = g // 3
        c = g % 3
        left = jnp.concatenate([ft[:, a * CELLS : (a + 4) * CELLS] for a in range(3)], axis=0)
        right = jnp.concatenate([taps_g(c, p, b) for p in range(1, 5)], axis=0)
        pk[u] = jnp.dot(left, right, preferred_element_type=F32).astype(BF).reshape(3, NY, NX, 16, C)

        @pl.when(odd == 0)
        def _():
            y1(n).start()

        @pl.when(odd == 1)
        def _():
            for d in range(1, NX):
                x1(n, d).start()

        return carry

    lax.fori_loop(0, 9, terms, 0)

    def sum_x1(n):
        total = pk[2 * n + 1, :, :, x].astype(F32)
        for d in range(1, NX):
            x1(n, d).wait_recv()
            total = total + xr1[n, d - 1].astype(F32)
        total = total.astype(BF)
        for k in range(NY):
            s1x[n, k] = total[:, k]
        y2(n).start()

    def sum_y1(n):
        y1(n).wait_recv()
        total = (pk[2 * n, :, y].astype(F32) + yr1[n].astype(F32)).astype(BF)
        for k in range(NX):
            s1y[n, k] = total[:, k]
        for d in range(1, NX):
            x2(n, d).start()

    def sum_1(n, carry):
        sum_y1(n)

        @pl.when(n < len(X_SET))
        def _():
            sum_x1(n)

        return carry

    def sum_x2(n):
        y2(n).wait_recv()
        total = s1x[n, y].astype(F32) + yr2[n].astype(F32)
        s2x[n * 48 : (n + 1) * 48, :] = total.astype(BF).reshape(48, C)

    def sum_y2(n):
        total = s1y[n, x].astype(F32)
        for d in range(1, NX):
            x2(n, d).wait_recv()
            total = total + xr2[n, d - 1].astype(F32)
        s2y[n * 48 : (n + 1) * 48, :] = total.astype(BF).reshape(48, C)

    def ordered(perm, rows, out):
        out[...] = jnp.dot(perm[...], rows[...], preferred_element_type=F32).astype(BF).reshape(out.shape)

    def last(perm, rows, zs, zr, ss, rs):
        ordered(perm, rows, zs)
        return [
            start(zs.at[lax.rem(z + d, NZ)], zr.at[d - 1], ss.at[d - 1], rs.at[d - 1], z_peers[d - 1])
            for d in range(1, NZ)
        ]

    def input_part(n, carry):
        i = n // 3
        a = n % 3
        left = jnp.concatenate([taps_g(c, first + i + 1 - a, b) for b in range(3) for c in range(3)], axis=1)
        right = jnp.concatenate([kv[9 * a + u] for u in range(9)], axis=1)

        @pl.when(a == 0)
        def _():
            acc[i] = jnp.zeros((CELLS, C), F32)

        acc[i] += lax.dot_general(left, right, NT, preferred_element_type=F32)
        return carry

    row = lax.broadcasted_iota(jnp.int32, (C, C), 0)
    col = lax.broadcasted_iota(jnp.int32, (C, C), 1)
    for perm, groups, shift in ((permx, X_SET, BX), (permy, Y_SET, BY)):
        n = len(groups)
        block = lax.div(row, shift)
        q = row - block * shift
        a = jnp.where(q >= 2 * n, 1, 0) + jnp.where(q >= 4 * n, 1, 0)
        rest = q - 2 * n * a
        source = ((rest >> 1) * 3 + a) * 16 + block * 2 + (rest & 1)
        hot = jnp.where((source == col) & (q < 6 * n), 1.0, 0.0).astype(BF)
        perm[...] = hot[: 8 * shift]
    s2x[...] = jnp.zeros_like(s2x)
    s2y[...] = jnp.zeros_like(s2y)

    g_out.wait_recv()
    spread_g(5 * core)
    lax.fori_loop(0, 6, input_part, 0)
    for i in range(2):
        low, high = acc[i, :, :HALF], acc[i, :, HALF:]
        own[i] = jnp.where(l == 0, low, high)
        igs[i] = jnp.where(l == 0, high, low).astype(BF)
    lax.fori_loop(0, len(Y_SET), sum_1, 0)
    ig_copies = [start(igs.at[i], igr.at[i], i_s.at[i], i_r.at[i], chan_peer) for i in range(2)]
    for n in range(4):
        sum_x2(n)
    copies_x = last(permx, s2x, zsx, zrx, zx_s, zx_r)
    for n in range(5):
        sum_y2(n)
    copies_y = last(permy, s2y, zsy, zry, zy_s, zy_r)

    def final(groups, copies, mine, taken):
        total = mine.astype(F32)
        for d, copy in enumerate(copies):
            copy.wait_recv()
            total = total + taken[d].astype(F32)
        n = len(groups)
        for a in range(3):
            kg_sum[a * 9 + groups[0] : a * 9 + groups[0] + n] = total[a * 2 * n : (a + 1) * 2 * n].reshape(n, 2, C)

    out_copies = []
    for i, copy in enumerate(ig_copies):
        copy.wait_recv()
        ig_sum[i] = (own[i] + igr[i].astype(F32)).astype(BF)
        out_copies.append(pltpu.make_async_copy(ig_sum.at[i], ig_out.at[i], loc.at[5 + i]))
        out_copies[-1].start()
    final(Y_SET, copies_y, zsy[z], zry)
    final(X_SET, copies_x, zsx[z], zrx)
    out_copies.append(pltpu.make_async_copy(kg_sum, kg_out, loc.at[7]))
    out_copies[-1].start()
    for copy in out_copies:
        copy.wait()

    for copy in sent:
        copy.wait_send()

    def drain(n, carry):
        y1(n).wait_send()
        for d in range(1, NX):
            x2(n, d).wait_send()

        @pl.when(n < len(X_SET))
        def _():
            y2(n).wait_send()
            for d in range(1, NX):
                x1(n, d).wait_send()

        return carry

    lax.fori_loop(0, len(Y_SET), drain, 0)


def copy_out(ig, kg, ig_out, kg_out, ig_held, kg_held, sem):
    steps = []
    for i in range(2):
        for h in range(2):
            part = (i, pl.ds(h * (CELLS // 2), CELLS // 2))
            steps.append((ig.at[part], ig_held.at[part], ig_out.at[part]))
    steps.append((kg, kg_held, kg_out))
    copies = [
        (pltpu.make_async_copy(a, b, sem.at[0, n]), pltpu.make_async_copy(b, c, sem.at[1, n]))
        for n, (a, b, c) in enumerate(steps)
    ]
    for inward, _ in copies:
        inward.start()
    for inward, outward in copies:
        inward.wait()
        outward.start()
    for _, outward in copies:
        outward.wait()


def shards(features, kernel, cotangent):
    taps = jnp.transpose(kernel, (1, 0, 2))
    dma = pltpu.SemaphoreType.DMA
    nx, ny = len(X_SET), len(Y_SET)
    pairs = [(3,), (3,), (nx, 3), (nx,), (ny,), (ny, 3), (7,), (7,), (2,)]
    sems = [dma((8,))]
    for shape in pairs:
        sems += [dma(shape), dma(shape)]
    whole = pl.BlockSpec(memory_space=pl.ANY)
    input_grad, kernel_grad = pl.pallas_call(
        fused,
        name="conv_grads",
        out_shape=(
            jax.ShapeDtypeStruct((2, CELLS, HALF), BF),
            jax.ShapeDtypeStruct((27, 2, C), F32),
        ),
        in_specs=[whole] * 3,
        out_specs=(whole, whole),
        scratch_shapes=[
            pltpu.VMEM((27, C, C), BF),
            pltpu.VMEM((6, CELLS, C), BF),
            pltpu.VMEM((2, CELLS, C), BF),
            pltpu.VMEM((3, 4, HALO, C), BF),
            pltpu.VMEM((6, CELLS, C), BF),
            pltpu.VMEM((3, 6, SY + 2, SZ, C), BF),
            pltpu.VMEM((HALF, 6 * CELLS), BF),
            pltpu.VMEM((2, CELLS, C), F32),
            pltpu.VMEM((9, 3, NY, NX, 16, C), BF),
            pltpu.VMEM((nx, 3, 3, NY, 16, C), BF),
            pltpu.VMEM((nx, NY, 3, 16, C), BF),
            pltpu.VMEM((nx, 3, 16, C), BF),
            pltpu.VMEM((ny, 3, NX, 16, C), BF),
            pltpu.VMEM((ny, NX, 3, 16, C), BF),
            pltpu.VMEM((ny, 3, 3, 16, C), BF),
            pltpu.VMEM((C, C), BF),
            pltpu.VMEM((C, C), BF),
            pltpu.VMEM((NZ, BX, C), BF),
            pltpu.VMEM((NZ, BY, C), BF),
            pltpu.VMEM((NZ - 1, BX, C), BF),
            pltpu.VMEM((NZ - 1, BY, C), BF),
            pltpu.VMEM((2, CELLS, HALF), F32),
            pltpu.VMEM((2, CELLS, HALF), BF),
            pltpu.VMEM((2, CELLS, HALF), BF),
            pltpu.VMEM((8 * BX, C), BF),
            pltpu.VMEM((8 * BY, C), BF),
            pltpu.VMEM((HALF, C), BF),
            pltpu.VMEM((2, CELLS, HALF), BF),
            pltpu.VMEM((27, 2, C), F32),
            *sems,
        ],
        compiler_params=pltpu.CompilerParams(
            collective_id=0, has_side_effects=True, vmem_limit_bytes=58 * 1024 * 1024
        ),
        cost_estimate=pl.CostEstimate(flops=11_000_000_000, bytes_accessed=6_000_000, transcendentals=300_000),
    )(features.reshape(2, CELLS, C), taps, cotangent.reshape(2, CELLS, C))
    input_grad, kernel_grad = pl.pallas_call(
        copy_out,
        name="copy_out",
        out_shape=(
            jax.ShapeDtypeStruct((2, CELLS, HALF), BF),
            jax.ShapeDtypeStruct((27, 2, C), F32),
        ),
        in_specs=[whole] * 2,
        out_specs=(whole, whole),
        scratch_shapes=[
            pltpu.VMEM((2, CELLS, HALF), BF),
            pltpu.VMEM((27, 2, C), F32),
            dma((2, 5)),
        ],
        compiler_params=pltpu.CompilerParams(vmem_limit_bytes=60 * 1024 * 1024),
    )(input_grad, kernel_grad)
    return (
        input_grad.reshape(2, SY, SZ, HALF),
        jnp.transpose(kernel_grad, (1, 0, 2)),
    )


def solution(mesh):
    placed = (P("space", None, None, None), P(None, None, "chan"), P("space", None, None, "chan"))
    return jax.shard_map(
        shards,
        mesh=mesh,
        in_specs=placed,
        out_specs=(P("space", None, None, "chan"), P("space", None, "chan")),
        check_vma=False,
    )
```

```python
import jax
import jax.numpy as jnp
from jax import lax
from jax.experimental import pallas as pl
from jax.experimental.pallas import tpu as pltpu
from jax.sharding import PartitionSpec as P

BF = jnp.bfloat16
F32 = jnp.float32
MESH = pl.DeviceIdType.MESH

NY, NX, NZ = 2, 4, 8
SY, SZ, C = 16, 32, 256
CELLS = SY * SZ
HALO = CELLS + 2 * SZ
HALF = 128

Y_SET = (0, 1, 2, 3, 4)
X_SET = (5, 6, 7, 8)

NT = (((1,), (1,)), ((), ()))


def block_rows(groups):
    return -(-6 * len(groups) // 16) * 16


BX, BY = block_rows(X_SET), block_rows(Y_SET)


def device(y, x, z, core):
    return ((y * NX + x) * NZ + z) * 2 + core


def spread(plane, sign, store):
    wide = plane.reshape(SY, SZ, C)
    wide32 = wide.astype(F32)
    for ci, c in enumerate((-1, 0, 1)):
        part = wide if c == 0 else pltpu.roll(wide32, (sign * c) % SZ, 1).astype(BF)
        store(ci, part.reshape(CELLS, C))


def fused(
    feat, kern, cot, ig_out, kg_out,
    kv, fb, ct, fs, pr, ps, ft, acc, pk,
    xr1, s1x, yr2, yr1, s1y, xr2, s2x, s2y, zsx, zsy, zrx, zry,
    own, igs, igr, permx, permy, sel,
    ig_sum, kg_sum,
    loc, f_s, f_r, g_s, g_r, x1_s, x1_r, y2_s, y2_r, y1_s, y1_r, x2_s, x2_r,
    zx_s, zx_r, zy_s, zy_r, i_s, i_r,
):
    s = lax.axis_index("space")
    l = lax.axis_index("chan")
    core = lax.rem(s, 2)
    z = lax.rem(lax.div(s, 2), NZ)
    x = lax.rem(lax.div(s, 2 * NZ), NX)
    y = lax.div(s, 2 * NZ * NX)
    count = 2 * NZ * NX * NY

    partner = (device(y, x, z, 1 - core), l)
    outer = (lax.rem(s + 2 * core - 1 + count, count), l)
    x_peers = [(device(y, lax.rem(x + d, NX), z, core), l) for d in range(1, NX)]
    y_peer = (device(1 - y, x, z, core), l)
    z_peers = [(device(y, x, lax.rem(z + d, NZ), core), l) for d in range(1, NZ)]
    chan_peer = (s, 1 - l)

    sent = []

    def send(src, dst, ss, rs, to):
        copy = pltpu.make_async_remote_copy(
            src_ref=src, dst_ref=dst, send_sem=ss, recv_sem=rs, device_id=to, device_id_type=MESH
        )
        sent.append(copy)
        return copy

    def start(*args):
        copy = send(*args)
        copy.start()
        return copy

    first = 1 + 2 * core
    here = pl.ds(first, 2)
    load_f = pltpu.make_async_copy(feat, fb.at[here], loc.at[0])
    load_f.start()
    load_k = []
    for n, t0 in enumerate((9, 0, 18)):
        part = pl.ds(t0, 9)
        load_k.append(pltpu.make_async_copy(kern.at[part], kv.at[part], loc.at[1 + n]))
    for copy in load_k:
        copy.start()
    load_c = pltpu.make_async_copy(cot, ct, loc.at[4])

    barrier = pltpu.get_barrier_semaphore()
    greeted = [partner, outer, *x_peers, y_peer, *z_peers, chan_peer]
    for peer in greeted:
        pl.semaphore_signal(barrier, inc=1, device_id=peer, device_id_type=MESH)

    pl.semaphore_wait(barrier, len(greeted))

    f_out = start(feat.at[core], fb.at[5 * (1 - core)], f_s.at[0], f_r.at[0], outer)
    f_pair = start(feat, fb.at[here], f_s.at[1], f_r.at[1], partner)

    def spread_f(slot, plane):
        def store(ci, part):
            fs[ci, slot, SZ : SZ + CELLS, :] = part
            fs[ci, slot, 0:SZ, :] = part[CELLS - SZ :]
            fs[ci, slot, SZ + CELLS :, :] = part[:SZ]

        spread(plane, -1, store)

    def spread_g(g):
        def store(ci, part):
            part = part.reshape(SY, SZ, C)
            ps[ci, g, 1 : SY + 1] = part
            ps[ci, g, 0] = part[SY - 1]
            ps[ci, g, SY + 1] = part[0]

        spread(pr[g], 1, store)

    def taps_g(c, g, b):
        return ps[c, g, pl.ds(2 - b, SY)].reshape(CELLS, C)

    def taps_f(slot):
        return jnp.concatenate(
            [fs[c, slot, b * SZ : b * SZ + CELLS, :] for b in range(3) for c in range(3)], axis=1
        )

    def times(slot, t0):
        return jnp.dot(taps_f(slot), kv[pl.ds(t0, 9)].reshape(9 * C, C), preferred_element_type=F32)

    row = lax.broadcasted_iota(jnp.int32, (HALF, C), 0)
    col = lax.broadcasted_iota(jnp.int32, (HALF, C), 1)
    sel[...] = jnp.where((row >> 1) * 4 + core * 2 + (row & 1) == col, 1.0, 0.0).astype(BF)

    load_f.wait()
    for i in range(2):
        spread_f(1 + i, fb[first + i])
    acc[...] = jnp.zeros_like(acc)

    def epilogue(i, g):
        def body(n, carry):
            rows = pl.ds(pl.multiple_of(n * 64, 64), 64)
            pre = acc[i, rows, :]
            sig = 1.0 / (1.0 + jnp.exp(-pre))
            pr[g, rows, :] = (ct[i, rows, :].astype(F32) * sig * (1.0 + pre * (1.0 - sig))).astype(BF)
            return carry

        lax.fori_loop(0, CELLS // 64, body, 0)

    def features_t(g, carry):
        cols = pl.ds(pl.multiple_of(g * CELLS, CELLS), CELLS)
        ft[:, cols] = lax.dot_general(sel[...], fb[g], NT, preferred_element_type=F32).astype(BF)
        return carry

    inner = 1 - core
    side = 3 * inner
    g_inner, g_outer, g_far = 2 + core, 1 + 3 * core, 5 * core
    g_side = 2 * core + side
    f_relay = send(fb.at[g_far], fb.at[g_far], f_s.at[2], f_r.at[2], partner)
    g_pair0 = send(pr.at[g_inner], pr.at[g_inner], g_s.at[0], g_r.at[0], partner)
    g_pair1 = send(pr.at[g_outer], pr.at[g_outer], g_s.at[1], g_r.at[1], partner)
    g_out = send(pr.at[g_outer], pr.at[5 * inner], g_s.at[2], g_r.at[2], outer)

    def forward(n, carry):
        late = n // 4
        m = n % 4
        slot = (1 - late) * (1 + n % 2) + late * ((1 - m) * side + m * 3 * core)
        t0 = (1 - late) * (9 + (n // 2) * (18 * (n % 2) - 9)) + late * 18 * ((1 - m) * inner + m * core)
        i = (1 - late) * ((n % 2 + n // 2) % 2) + late * ((1 - m) * inner + m * core)

        @pl.when(n == 0)
        def _():
            load_k[0].wait()

        @pl.when(n == 2)
        def _():
            load_k[1].wait()
            load_c.start()

        @pl.when(n == 3)
        def _():
            load_k[2].wait()

        @pl.when(n == 4)
        def _():
            load_c.wait()
            f_pair.wait_recv()

        @pl.when(n == 5)
        def _():
            lax.fori_loop(1, 5, features_t, 0)
            spread_g(g_inner)
            g_pair0.wait_recv()
            spread_g(3 - core)
            f_out.wait_recv()
            f_relay.start()

        @pl.when(n >= 4)
        def _():
            spread_f(slot, fb[2 * core + slot])

        acc[i] += times(slot, t0)

        @pl.when(n >= 4)
        def _():
            epilogue(i, first + i)

        @pl.when(n == 4)
        def _():
            g_pair0.start()

        @pl.when(n == 5)
        def _():
            g_pair1.start()
            g_out.start()

        return carry

    lax.fori_loop(0, 6, forward, 0)
    spread_g(g_outer)
    features_t(g_far, 0)
    f_relay.wait_recv()
    features_t(5 * inner, 0)
    g_pair1.wait_recv()
    spread_g(4 - 3 * core)

    def remote(src, dst, ss, rs, to):
        return pltpu.make_async_remote_copy(
            src_ref=src, dst_ref=dst, send_sem=ss, recv_sem=rs, device_id=to, device_id_type=MESH
        )

    def x1(n, d):
        mine = pk.at[2 * n + 1, :, :, lax.rem(x + d, NX)]
        return remote(mine, xr1.at[n, d - 1], x1_s.at[n, d - 1], x1_r.at[n, d - 1], x_peers[d - 1])

    def y1(n):
        return remote(pk.at[2 * n, :, 1 - y], yr1.at[n], y1_s.at[n], y1_r.at[n], y_peer)

    def x2(n, d):
        mine = s1y.at[n, lax.rem(x + d, NX)]
        return remote(mine, xr2.at[n, d - 1], x2_s.at[n, d - 1], x2_r.at[n, d - 1], x_peers[d - 1])

    def y2(n):
        return remote(s1x.at[n, 1 - y], yr2.at[n], y2_s.at[n], y2_r.at[n], y_peer)

    def terms(u, carry):
        odd = u % 2
        n = u // 2
        g = n + len(Y_SET) * odd
        b = g // 3
        c = g % 3
        left = jnp.concatenate([ft[:, a * CELLS : (a + 4) * CELLS] for a in range(3)], axis=0)
        right = jnp.concatenate([taps_g(c, p, b) for p in range(1, 5)], axis=0)
        pk[u] = jnp.dot(left, right, preferred_element_type=F32).astype(BF).reshape(3, NY, NX, 16, C)

        @pl.when(odd == 0)
        def _():
            y1(n).start()

        @pl.when(odd == 1)
        def _():
            for d in range(1, NX):
                x1(n, d).start()

        return carry

    lax.fori_loop(0, 9, terms, 0)

    def sum_x1(n):
        total = pk[2 * n + 1, :, :, x].astype(F32)
        for d in range(1, NX):
            x1(n, d).wait_recv()
            total = total + xr1[n, d - 1].astype(F32)
        total = total.astype(BF)
        for k in range(NY):
            s1x[n, k] = total[:, k]
        y2(n).start()

    def sum_y1(n):
        y1(n).wait_recv()
        total = (pk[2 * n, :, y].astype(F32) + yr1[n].astype(F32)).astype(BF)
        for k in range(NX):
            s1y[n, k] = total[:, k]
        for d in range(1, NX):
            x2(n, d).start()

    def sum_1(n, carry):
        @pl.when(n < len(X_SET))
        def _():
            sum_x1(n)

        sum_y1(n)

        return carry

    def sum_x2(n):
        y2(n).wait_recv()
        total = s1x[n, y].astype(F32) + yr2[n].astype(F32)
        s2x[n * 48 : (n + 1) * 48, :] = total.astype(BF).reshape(48, C)

    def sum_y2(n):
        total = s1y[n, x].astype(F32)
        for d in range(1, NX):
            x2(n, d).wait_recv()
            total = total + xr2[n, d - 1].astype(F32)
        s2y[n * 48 : (n + 1) * 48, :] = total.astype(BF).reshape(48, C)

    def ordered(perm, rows, out):
        out[...] = jnp.dot(perm[...], rows[...], preferred_element_type=F32).astype(BF).reshape(out.shape)

    def last(perm, rows, zs, zr, ss, rs):
        ordered(perm, rows, zs)
        return [
            start(zs.at[lax.rem(z + d, NZ)], zr.at[d - 1], ss.at[d - 1], rs.at[d - 1], z_peers[d - 1])
            for d in range(1, NZ)
        ]

    def input_part(n, carry):
        i = n // 3
        a = n % 3
        left = jnp.concatenate([taps_g(c, first + i + 1 - a, b) for b in range(3) for c in range(3)], axis=1)
        right = jnp.concatenate([kv[9 * a + u] for u in range(9)], axis=1)

        @pl.when(a == 0)
        def _():
            acc[i] = jnp.zeros((CELLS, C), F32)

        acc[i] += lax.dot_general(left, right, NT, preferred_element_type=F32)
        return carry

    row = lax.broadcasted_iota(jnp.int32, (C, C), 0)
    col = lax.broadcasted_iota(jnp.int32, (C, C), 1)
    for perm, groups, shift in ((permx, X_SET, BX), (permy, Y_SET, BY)):
        n = len(groups)
        block = lax.div(row, shift)
        q = row - block * shift
        a = jnp.where(q >= 2 * n, 1, 0) + jnp.where(q >= 4 * n, 1, 0)
        rest = q - 2 * n * a
        source = ((rest >> 1) * 3 + a) * 16 + block * 2 + (rest & 1)
        hot = jnp.where((source == col) & (q < 6 * n), 1.0, 0.0).astype(BF)
        perm[...] = hot[: 8 * shift]
    s2x[...] = jnp.zeros_like(s2x)
    s2y[...] = jnp.zeros_like(s2y)

    g_out.wait_recv()
    spread_g(5 * core)
    lax.fori_loop(0, 6, input_part, 0)
    for i in range(2):
        low, high = acc[i, :, :HALF], acc[i, :, HALF:]
        own[i] = jnp.where(l == 0, low, high)
        igs[i] = jnp.where(l == 0, high, low).astype(BF)
    lax.fori_loop(0, len(Y_SET), sum_1, 0)
    ig_copies = [start(igs.at[i], igr.at[i], i_s.at[i], i_r.at[i], chan_peer) for i in range(2)]
    for n in range(4):
        sum_x2(n)
    copies_x = last(permx, s2x, zsx, zrx, zx_s, zx_r)
    for n in range(5):
        sum_y2(n)
    copies_y = last(permy, s2y, zsy, zry, zy_s, zy_r)

    def final(groups, copies, mine, taken):
        total = mine.astype(F32)
        for d, copy in enumerate(copies):
            copy.wait_recv()
            total = total + taken[d].astype(F32)
        n = len(groups)
        for a in range(3):
            kg_sum[a * 9 + groups[0] : a * 9 + groups[0] + n] = total[a * 2 * n : (a + 1) * 2 * n].reshape(n, 2, C)

    out_copies = []
    for i, copy in enumerate(ig_copies):
        copy.wait_recv()
        ig_sum[i] = (own[i] + igr[i].astype(F32)).astype(BF)
        out_copies.append(pltpu.make_async_copy(ig_sum.at[i], ig_out.at[i], loc.at[5 + i]))
        out_copies[-1].start()
    final(Y_SET, copies_y, zsy[z], zry)
    final(X_SET, copies_x, zsx[z], zrx)
    out_copies.append(pltpu.make_async_copy(kg_sum, kg_out, loc.at[7]))
    out_copies[-1].start()
    for copy in out_copies:
        copy.wait()

    for copy in sent:
        copy.wait_send()

    def drain(n, carry):
        y1(n).wait_send()
        for d in range(1, NX):
            x2(n, d).wait_send()

        @pl.when(n < len(X_SET))
        def _():
            y2(n).wait_send()
            for d in range(1, NX):
                x1(n, d).wait_send()

        return carry

    lax.fori_loop(0, len(Y_SET), drain, 0)


def copy_out(ig, kg, ig_out, kg_out, ig_held, kg_held, sem):
    steps = []
    for i in range(2):
        for h in range(2):
            part = (i, pl.ds(h * (CELLS // 2), CELLS // 2))
            steps.append((ig.at[part], ig_held.at[part], ig_out.at[part]))
    steps.append((kg, kg_held, kg_out))
    copies = [
        (pltpu.make_async_copy(a, b, sem.at[0, n]), pltpu.make_async_copy(b, c, sem.at[1, n]))
        for n, (a, b, c) in enumerate(steps)
    ]
    for inward, _ in copies:
        inward.start()
    for inward, outward in copies:
        inward.wait()
        outward.start()
    for _, outward in copies:
        outward.wait()


def shards(features, kernel, cotangent):
    taps = jnp.transpose(kernel, (1, 0, 2))
    dma = pltpu.SemaphoreType.DMA
    nx, ny = len(X_SET), len(Y_SET)
    pairs = [(3,), (3,), (nx, 3), (nx,), (ny,), (ny, 3), (7,), (7,), (2,)]
    sems = [dma((8,))]
    for shape in pairs:
        sems += [dma(shape), dma(shape)]
    whole = pl.BlockSpec(memory_space=pl.ANY)
    input_grad, kernel_grad = pl.pallas_call(
        fused,
        name="conv_grads",
        out_shape=(
            jax.ShapeDtypeStruct((2, CELLS, HALF), BF),
            jax.ShapeDtypeStruct((27, 2, C), F32),
        ),
        in_specs=[whole] * 3,
        out_specs=(whole, whole),
        scratch_shapes=[
            pltpu.VMEM((27, C, C), BF),
            pltpu.VMEM((6, CELLS, C), BF),
            pltpu.VMEM((2, CELLS, C), BF),
            pltpu.VMEM((3, 4, HALO, C), BF),
            pltpu.VMEM((6, CELLS, C), BF),
            pltpu.VMEM((3, 6, SY + 2, SZ, C), BF),
            pltpu.VMEM((HALF, 6 * CELLS), BF),
            pltpu.VMEM((2, CELLS, C), F32),
            pltpu.VMEM((9, 3, NY, NX, 16, C), BF),
            pltpu.VMEM((nx, 3, 3, NY, 16, C), BF),
            pltpu.VMEM((nx, NY, 3, 16, C), BF),
            pltpu.VMEM((nx, 3, 16, C), BF),
            pltpu.VMEM((ny, 3, NX, 16, C), BF),
            pltpu.VMEM((ny, NX, 3, 16, C), BF),
            pltpu.VMEM((ny, 3, 3, 16, C), BF),
            pltpu.VMEM((C, C), BF),
            pltpu.VMEM((C, C), BF),
            pltpu.VMEM((NZ, BX, C), BF),
            pltpu.VMEM((NZ, BY, C), BF),
            pltpu.VMEM((NZ - 1, BX, C), BF),
            pltpu.VMEM((NZ - 1, BY, C), BF),
            pltpu.VMEM((2, CELLS, HALF), F32),
            pltpu.VMEM((2, CELLS, HALF), BF),
            pltpu.VMEM((2, CELLS, HALF), BF),
            pltpu.VMEM((8 * BX, C), BF),
            pltpu.VMEM((8 * BY, C), BF),
            pltpu.VMEM((HALF, C), BF),
            pltpu.VMEM((2, CELLS, HALF), BF),
            pltpu.VMEM((27, 2, C), F32),
            *sems,
        ],
        compiler_params=pltpu.CompilerParams(
            collective_id=0, has_side_effects=True, vmem_limit_bytes=58 * 1024 * 1024
        ),
        cost_estimate=pl.CostEstimate(flops=11_000_000_000, bytes_accessed=6_000_000, transcendentals=300_000),
    )(features.reshape(2, CELLS, C), taps, cotangent.reshape(2, CELLS, C))
    input_grad, kernel_grad = pl.pallas_call(
        copy_out,
        name="copy_out",
        out_shape=(
            jax.ShapeDtypeStruct((2, CELLS, HALF), BF),
            jax.ShapeDtypeStruct((27, 2, C), F32),
        ),
        in_specs=[whole] * 2,
        out_specs=(whole, whole),
        scratch_shapes=[
            pltpu.VMEM((2, CELLS, HALF), BF),
            pltpu.VMEM((27, 2, C), F32),
            dma((2, 5)),
        ],
        compiler_params=pltpu.CompilerParams(vmem_limit_bytes=60 * 1024 * 1024),
    )(input_grad, kernel_grad)
    return (
        input_grad.reshape(2, SY, SZ, HALF),
        jnp.transpose(kernel_grad, (1, 0, 2)),
    )


def solution(mesh):
    placed = (P("space", None, None, None), P(None, None, "chan"), P("space", None, None, "chan"))
    return jax.shard_map(
        shards,
        mesh=mesh,
        in_specs=placed,
        out_specs=(P("space", None, None, "chan"), P("space", None, "chan")),
        check_vma=False,
    )
```

```python
import jax
import jax.numpy as jnp
from jax import lax
from jax.experimental import pallas as pl
from jax.experimental.pallas import tpu as pltpu
from jax.sharding import PartitionSpec as P

BF = jnp.bfloat16
F32 = jnp.float32
MESH = pl.DeviceIdType.MESH

NY, NX, NZ = 2, 4, 8
SY, SZ, C = 16, 32, 256
CELLS = SY * SZ
HALO = CELLS + 2 * SZ
HALF = 128

Y_SET = (0, 1, 2, 3, 4)
X_SET = (5, 6, 7, 8)

NT = (((1,), (1,)), ((), ()))


def block_rows(groups):
    return -(-6 * len(groups) // 16) * 16


BX, BY = block_rows(X_SET), block_rows(Y_SET)


def device(y, x, z, core):
    return ((y * NX + x) * NZ + z) * 2 + core


def spread(plane, sign, store):
    wide = plane.reshape(SY, SZ, C)
    wide32 = wide.astype(F32)
    for ci, c in enumerate((-1, 0, 1)):
        part = wide if c == 0 else pltpu.roll(wide32, (sign * c) % SZ, 1).astype(BF)
        store(ci, part.reshape(CELLS, C))


def fused(
    feat, kern, cot, ig_out, kg_out,
    kv, fb, ct, fs, pr, ps, ft, acc, pk,
    xr1, s1x, yr2, yr1, s1y, xr2, s2x, s2y, zsx, zsy, zrx, zry,
    own, igs, igr, permx, permy, sel,
    ig_sum, kg_sum,
    loc, f_s, f_r, g_s, g_r, x1_s, x1_r, y2_s, y2_r, y1_s, y1_r, x2_s, x2_r,
    zx_s, zx_r, zy_s, zy_r, i_s, i_r,
):
    s = lax.axis_index("space")
    l = lax.axis_index("chan")
    core = lax.rem(s, 2)
    z = lax.rem(lax.div(s, 2), NZ)
    x = lax.rem(lax.div(s, 2 * NZ), NX)
    y = lax.div(s, 2 * NZ * NX)
    count = 2 * NZ * NX * NY

    partner = (device(y, x, z, 1 - core), l)
    outer = (lax.rem(s + 2 * core - 1 + count, count), l)
    x_peers = [(device(y, lax.rem(x + d, NX), z, core), l) for d in range(1, NX)]
    y_peer = (device(1 - y, x, z, core), l)
    z_peers = [(device(y, x, lax.rem(z + d, NZ), core), l) for d in range(1, NZ)]
    chan_peer = (s, 1 - l)

    sent = []

    def send(src, dst, ss, rs, to):
        copy = pltpu.make_async_remote_copy(
            src_ref=src, dst_ref=dst, send_sem=ss, recv_sem=rs, device_id=to, device_id_type=MESH
        )
        sent.append(copy)
        return copy

    def start(*args):
        copy = send(*args)
        copy.start()
        return copy

    first = 1 + 2 * core
    here = pl.ds(first, 2)
    load_f = pltpu.make_async_copy(feat, fb.at[here], loc.at[0])
    load_f.start()
    load_k = []
    for n, t0 in enumerate((9, 0, 18)):
        part = pl.ds(t0, 9)
        load_k.append(pltpu.make_async_copy(kern.at[part], kv.at[part], loc.at[1 + n]))
    for copy in load_k:
        copy.start()
    load_c = pltpu.make_async_copy(cot, ct, loc.at[4])
    load_c.start()

    barrier = pltpu.get_barrier_semaphore()
    greeted = [partner, outer, *x_peers, y_peer, *z_peers, chan_peer]
    for peer in greeted:
        pl.semaphore_signal(barrier, inc=1, device_id=peer, device_id_type=MESH)

    pl.semaphore_wait(barrier, len(greeted))

    f_out = start(feat.at[core], fb.at[5 * (1 - core)], f_s.at[0], f_r.at[0], outer)
    f_pair = start(feat, fb.at[here], f_s.at[1], f_r.at[1], partner)

    def spread_f(slot, plane):
        def store(ci, part):
            fs[ci, slot, SZ : SZ + CELLS, :] = part
            fs[ci, slot, 0:SZ, :] = part[CELLS - SZ :]
            fs[ci, slot, SZ + CELLS :, :] = part[:SZ]

        spread(plane, -1, store)

    def spread_g(g):
        def store(ci, part):
            part = part.reshape(SY, SZ, C)
            ps[ci, g, 1 : SY + 1] = part
            ps[ci, g, 0] = part[SY - 1]
            ps[ci, g, SY + 1] = part[0]

        spread(pr[g], 1, store)

    def taps_g(c, g, b):
        return ps[c, g, pl.ds(2 - b, SY)].reshape(CELLS, C)

    def taps_f(slot):
        return jnp.concatenate(
            [fs[c, slot, b * SZ : b * SZ + CELLS, :] for b in range(3) for c in range(3)], axis=1
        )

    def times(slot, t0):
        return jnp.dot(taps_f(slot), kv[pl.ds(t0, 9)].reshape(9 * C, C), preferred_element_type=F32)

    row = lax.broadcasted_iota(jnp.int32, (HALF, C), 0)
    col = lax.broadcasted_iota(jnp.int32, (HALF, C), 1)
    sel[...] = jnp.where((row >> 1) * 4 + core * 2 + (row & 1) == col, 1.0, 0.0).astype(BF)

    load_f.wait()
    for i in range(2):
        spread_f(1 + i, fb[first + i])
    acc[...] = jnp.zeros_like(acc)

    def epilogue(i, g):
        def body(n, carry):
            rows = pl.ds(pl.multiple_of(n * 64, 64), 64)
            pre = acc[i, rows, :]
            sig = 1.0 / (1.0 + jnp.exp(-pre))
            pr[g, rows, :] = (ct[i, rows, :].astype(F32) * sig * (1.0 + pre * (1.0 - sig))).astype(BF)
            return carry

        lax.fori_loop(0, CELLS // 64, body, 0)

    def features_t(g):
        cols = pl.ds(pl.multiple_of(g * CELLS, CELLS), CELLS)
        ft[:, cols] = lax.dot_general(sel[...], fb[g], NT, preferred_element_type=F32).astype(BF)

    inner = 1 - core
    side = 3 * inner
    g_inner, g_outer, g_far = 2 + core, 1 + 3 * core, 5 * core
    g_side = 2 * core + side
    f_relay = send(fb.at[g_far], fb.at[g_far], f_s.at[2], f_r.at[2], partner)
    g_pair0 = send(pr.at[g_inner], pr.at[g_inner], g_s.at[0], g_r.at[0], partner)
    g_pair1 = send(pr.at[g_outer], pr.at[g_outer], g_s.at[1], g_r.at[1], partner)
    g_out = send(pr.at[g_outer], pr.at[5 * inner], g_s.at[2], g_r.at[2], outer)

    def forward(n, carry):
        late = n // 4
        m = n % 4
        slot = (1 - late) * (1 + n % 2) + late * ((1 - m) * side + m * 3 * core)
        t0 = (1 - late) * (9 + (n // 2) * (18 * (n % 2) - 9)) + late * 18 * ((1 - m) * inner + m * core)
        i = (1 - late) * ((n % 2 + n // 2) % 2) + late * ((1 - m) * inner + m * core)

        @pl.when(n == 0)
        def _():
            load_k[0].wait()

        @pl.when(n == 2)
        def _():
            load_k[1].wait()

        @pl.when(n == 3)
        def _():
            load_k[2].wait()

        @pl.when(n == 4)
        def _():
            load_c.wait()
            f_pair.wait_recv()

        @pl.when(n == 5)
        def _():
            f_out.wait_recv()
            f_relay.start()

        @pl.when(n >= 4)
        def _():
            spread_f(slot, fb[2 * core + slot])

        acc[i] += times(slot, t0)

        @pl.when(n >= 4)
        def _():
            epilogue(i, first + i)

        @pl.when(n == 4)
        def _():
            g_pair0.start()

        @pl.when(n == 5)
        def _():
            g_pair1.start()
            g_out.start()

        return carry

    lax.fori_loop(0, 6, forward, 0)
    spread_g(g_inner)
    spread_g(g_outer)
    for g in range(1, 5):
        features_t(g)
    features_t(5 * core)
    f_relay.wait_recv()
    features_t(5 * (1 - core))
    g_pair0.wait_recv()
    spread_g(3 - core)
    g_pair1.wait_recv()
    spread_g(4 - 3 * core)

    def remote(src, dst, ss, rs, to):
        return pltpu.make_async_remote_copy(
            src_ref=src, dst_ref=dst, send_sem=ss, recv_sem=rs, device_id=to, device_id_type=MESH
        )

    def x1(n, d):
        mine = pk.at[2 * n + 1, :, :, lax.rem(x + d, NX)]
        return remote(mine, xr1.at[n, d - 1], x1_s.at[n, d - 1], x1_r.at[n, d - 1], x_peers[d - 1])

    def y1(n):
        return remote(pk.at[2 * n, :, 1 - y], yr1.at[n], y1_s.at[n], y1_r.at[n], y_peer)

    def x2(n, d):
        mine = s1y.at[n, lax.rem(x + d, NX)]
        return remote(mine, xr2.at[n, d - 1], x2_s.at[n, d - 1], x2_r.at[n, d - 1], x_peers[d - 1])

    def y2(n):
        return remote(s1x.at[n, 1 - y], yr2.at[n], y2_s.at[n], y2_r.at[n], y_peer)

    def terms(u, carry):
        odd = u % 2
        n = u // 2
        g = n + len(Y_SET) * odd
        b = g // 3
        c = g % 3
        left = jnp.concatenate([ft[:, a * CELLS : (a + 4) * CELLS] for a in range(3)], axis=0)
        right = jnp.concatenate([taps_g(c, p, b) for p in range(1, 5)], axis=0)
        pk[u] = jnp.dot(left, right, preferred_element_type=F32).astype(BF).reshape(3, NY, NX, 16, C)

        @pl.when(odd == 0)
        def _():
            y1(n).start()

        @pl.when(odd == 1)
        def _():
            for d in range(1, NX):
                x1(n, d).start()

        return carry

    lax.fori_loop(0, 9, terms, 0)

    def sum_x1(n):
        total = pk[2 * n + 1, :, :, x].astype(F32)
        for d in range(1, NX):
            x1(n, d).wait_recv()
            total = total + xr1[n, d - 1].astype(F32)
        total = total.astype(BF)
        for k in range(NY):
            s1x[n, k] = total[:, k]
        y2(n).start()

    def sum_y1(n):
        y1(n).wait_recv()
        total = (pk[2 * n, :, y].astype(F32) + yr1[n].astype(F32)).astype(BF)
        for k in range(NX):
            s1y[n, k] = total[:, k]
        for d in range(1, NX):
            x2(n, d).start()

    def sum_1(n, carry):
        sum_y1(n)

        @pl.when(n < len(X_SET))
        def _():
            sum_x1(n)

        return carry

    def sum_x2(n):
        y2(n).wait_recv()
        total = s1x[n, y].astype(F32) + yr2[n].astype(F32)
        s2x[n * 48 : (n + 1) * 48, :] = total.astype(BF).reshape(48, C)

    def sum_y2(n):
        total = s1y[n, x].astype(F32)
        for d in range(1, NX):
            x2(n, d).wait_recv()
            total = total + xr2[n, d - 1].astype(F32)
        s2y[n * 48 : (n + 1) * 48, :] = total.astype(BF).reshape(48, C)

    def ordered(perm, rows, out):
        out[...] = jnp.dot(perm[...], rows[...], preferred_element_type=F32).astype(BF).reshape(out.shape)

    def last(perm, rows, zs, zr, ss, rs):
        ordered(perm, rows, zs)
        copies = [
            send(zs.at[lax.rem(z + d, NZ)], zr.at[d - 1], ss.at[d - 1], rs.at[d - 1], z_peers[d - 1])
            for d in range(1, NZ)
        ]
        for d in (4, 3, 5, 2, 6, 1, 7):
            copies[d - 1].start()
        return copies

    def input_part(n, carry):
        i = n // 3
        a = n % 3
        left = jnp.concatenate([taps_g(c, first + i + 1 - a, b) for b in range(3) for c in range(3)], axis=1)
        right = jnp.concatenate([kv[9 * a + u] for u in range(9)], axis=1)

        @pl.when(a == 0)
        def _():
            acc[i] = jnp.zeros((CELLS, C), F32)

        acc[i] += lax.dot_general(left, right, NT, preferred_element_type=F32)
        return carry

    row = lax.broadcasted_iota(jnp.int32, (C, C), 0)
    col = lax.broadcasted_iota(jnp.int32, (C, C), 1)
    for perm, groups, shift in ((permx, X_SET, BX), (permy, Y_SET, BY)):
        n = len(groups)
        block = lax.div(row, shift)
        q = row - block * shift
        a = jnp.where(q >= 2 * n, 1, 0) + jnp.where(q >= 4 * n, 1, 0)
        rest = q - 2 * n * a
        source = ((rest >> 1) * 3 + a) * 16 + block * 2 + (rest & 1)
        hot = jnp.where((source == col) & (q < 6 * n), 1.0, 0.0).astype(BF)
        perm[...] = hot[: 8 * shift]
    s2x[...] = jnp.zeros_like(s2x)
    s2y[...] = jnp.zeros_like(s2y)

    g_out.wait_recv()
    spread_g(5 * core)
    lax.fori_loop(0, 6, input_part, 0)
    for i in range(2):
        low, high = acc[i, :, :HALF], acc[i, :, HALF:]
        own[i] = jnp.where(l == 0, low, high)
        igs[i] = jnp.where(l == 0, high, low).astype(BF)
    lax.fori_loop(0, len(Y_SET), sum_1, 0)
    ig_copies = [start(igs.at[i], igr.at[i], i_s.at[i], i_r.at[i], chan_peer) for i in range(2)]
    for n in range(4):
        sum_x2(n)
    copies_x = last(permx, s2x, zsx, zrx, zx_s, zx_r)
    for n in range(5):
        sum_y2(n)
    copies_y = last(permy, s2y, zsy, zry, zy_s, zy_r)

    def final(groups, copies, mine, taken):
        total = mine.astype(F32)
        for d, copy in enumerate(copies):
            copy.wait_recv()
            total = total + taken[d].astype(F32)
        n = len(groups)
        for a in range(3):
            kg_sum[a * 9 + groups[0] : a * 9 + groups[0] + n] = total[a * 2 * n : (a + 1) * 2 * n].reshape(n, 2, C)

    out_copies = []
    for i, copy in enumerate(ig_copies):
        copy.wait_recv()
        ig_sum[i] = (own[i] + igr[i].astype(F32)).astype(BF)
        out_copies.append(pltpu.make_async_copy(ig_sum.at[i], ig_out.at[i], loc.at[5 + i]))
        out_copies[-1].start()
    final(Y_SET, copies_y, zsy[z], zry)
    final(X_SET, copies_x, zsx[z], zrx)
    out_copies.append(pltpu.make_async_copy(kg_sum, kg_out, loc.at[7]))
    out_copies[-1].start()
    for copy in out_copies:
        copy.wait()

    for copy in sent:
        copy.wait_send()

    def drain(n, carry):
        y1(n).wait_send()
        for d in range(1, NX):
            x2(n, d).wait_send()

        @pl.when(n < len(X_SET))
        def _():
            y2(n).wait_send()
            for d in range(1, NX):
                x1(n, d).wait_send()

        return carry

    lax.fori_loop(0, len(Y_SET), drain, 0)


def copy_out(ig, kg, ig_out, kg_out, ig_held, kg_held, sem):
    steps = []
    for i in range(2):
        for h in range(2):
            part = (i, pl.ds(h * (CELLS // 2), CELLS // 2))
            steps.append((ig.at[part], ig_held.at[part], ig_out.at[part]))
    steps.append((kg, kg_held, kg_out))
    copies = [
        (pltpu.make_async_copy(a, b, sem.at[0, n]), pltpu.make_async_copy(b, c, sem.at[1, n]))
        for n, (a, b, c) in enumerate(steps)
    ]
    for inward, _ in copies:
        inward.start()
    for inward, outward in copies:
        inward.wait()
        outward.start()
    for _, outward in copies:
        outward.wait()


def shards(features, kernel, cotangent):
    taps = jnp.transpose(kernel, (1, 0, 2))
    dma = pltpu.SemaphoreType.DMA
    nx, ny = len(X_SET), len(Y_SET)
    pairs = [(3,), (3,), (nx, 3), (nx,), (ny,), (ny, 3), (7,), (7,), (2,)]
    sems = [dma((8,))]
    for shape in pairs:
        sems += [dma(shape), dma(shape)]
    whole = pl.BlockSpec(memory_space=pl.ANY)
    input_grad, kernel_grad = pl.pallas_call(
        fused,
        name="conv_grads",
        out_shape=(
            jax.ShapeDtypeStruct((2, CELLS, HALF), BF),
            jax.ShapeDtypeStruct((27, 2, C), F32),
        ),
        in_specs=[whole] * 3,
        out_specs=(whole, whole),
        scratch_shapes=[
            pltpu.VMEM((27, C, C), BF),
            pltpu.VMEM((6, CELLS, C), BF),
            pltpu.VMEM((2, CELLS, C), BF),
            pltpu.VMEM((3, 4, HALO, C), BF),
            pltpu.VMEM((6, CELLS, C), BF),
            pltpu.VMEM((3, 6, SY + 2, SZ, C), BF),
            pltpu.VMEM((HALF, 6 * CELLS), BF),
            pltpu.VMEM((2, CELLS, C), F32),
            pltpu.VMEM((9, 3, NY, NX, 16, C), BF),
            pltpu.VMEM((nx, 3, 3, NY, 16, C), BF),
            pltpu.VMEM((nx, NY, 3, 16, C), BF),
            pltpu.VMEM((nx, 3, 16, C), BF),
            pltpu.VMEM((ny, 3, NX, 16, C), BF),
            pltpu.VMEM((ny, NX, 3, 16, C), BF),
            pltpu.VMEM((ny, 3, 3, 16, C), BF),
            pltpu.VMEM((C, C), BF),
            pltpu.VMEM((C, C), BF),
            pltpu.VMEM((NZ, BX, C), BF),
            pltpu.VMEM((NZ, BY, C), BF),
            pltpu.VMEM((NZ - 1, BX, C), BF),
            pltpu.VMEM((NZ - 1, BY, C), BF),
            pltpu.VMEM((2, CELLS, HALF), F32),
            pltpu.VMEM((2, CELLS, HALF), BF),
            pltpu.VMEM((2, CELLS, HALF), BF),
            pltpu.VMEM((8 * BX, C), BF),
            pltpu.VMEM((8 * BY, C), BF),
            pltpu.VMEM((HALF, C), BF),
            pltpu.VMEM((2, CELLS, HALF), BF),
            pltpu.VMEM((27, 2, C), F32),
            *sems,
        ],
        compiler_params=pltpu.CompilerParams(
            collective_id=0, has_side_effects=True, vmem_limit_bytes=58 * 1024 * 1024
        ),
        cost_estimate=pl.CostEstimate(flops=11_000_000_000, bytes_accessed=6_000_000, transcendentals=300_000),
    )(features.reshape(2, CELLS, C), taps, cotangent.reshape(2, CELLS, C))
    input_grad, kernel_grad = pl.pallas_call(
        copy_out,
        name="copy_out",
        out_shape=(
            jax.ShapeDtypeStruct((2, CELLS, HALF), BF),
            jax.ShapeDtypeStruct((27, 2, C), F32),
        ),
        in_specs=[whole] * 2,
        out_specs=(whole, whole),
        scratch_shapes=[
            pltpu.VMEM((2, CELLS, HALF), BF),
            pltpu.VMEM((27, 2, C), F32),
            dma((2, 5)),
        ],
        compiler_params=pltpu.CompilerParams(vmem_limit_bytes=60 * 1024 * 1024),
    )(input_grad, kernel_grad)
    return (
        input_grad.reshape(2, SY, SZ, HALF),
        jnp.transpose(kernel_grad, (1, 0, 2)),
    )


def solution(mesh):
    placed = (P("space", None, None, None), P(None, None, "chan"), P("space", None, None, "chan"))
    return jax.shard_map(
        shards,
        mesh=mesh,
        in_specs=placed,
        out_specs=(P("space", None, None, "chan"), P("space", None, "chan")),
        check_vma=False,
    )
```
